128 devices in a mesh: blk: 128 (over x, z, y, core).
Axes of the slice: x: 4, y: 4, z: 4, core: 2. Of those that a mesh axis runs over, the one named last changes fastest.
Arguments:
- embeddings: bfloat16 [49152, 768], P('blk'), may hold values from -6 to 6
- log_norms: bfloat16 [49152], P('blk'), may hold values from 6.5 to 9.5
- destinations: int32 [49152, 1], P('blk'), may hold values from 0 to 127; in each aligned block of 384 rows (0 to 383, 384 to 767, ...) at most 5 rows name the same one
- centroids: bfloat16 [262144, 768], P('blk'), may hold values from -6 to 6
Outputs:
- new_centroids: bfloat16 [262144, 768], P('blk')
The draws below stay inside these ranges and needn't reach their ends.
Inputs may be any that keep to these rules, and one draw needn't show every extreme that they name: `destinations`: among the 384 rows of one reader, no device is named more than 5 times; some device is named exactly 5 times.
All inputs are finite; a program needn't handle non-finite values.
Results may differ from the reference program's by a relative error of at most 0.0042.
Values may be sent and summed in bfloat16 or wider, within the bound.
A program may use at most 64 MiB of HBM per device.

```python
import math
import jax
import jax.numpy as jnp
import numpy as np
from jax import lax

D = 768
PANEL = 2048
STOPS = 2
POOL = 384
CAP = 5
READ_ROWS = 49152
CENTROIDS = 262144
N_BLK = 128


def level_of(stream_key, shape, split, smallest, high):
    def one(dim, shards_of):
        draws = jax.random.uniform(jax.random.fold_in(jax.random.fold_in(stream_key, 6), dim), (shards_of,), jnp.float32, smallest / len(split), high / len(split))
        return jnp.repeat(jnp.exp(draws), shape[dim] // shards_of).reshape((-1,) + (1,) * (len(shape) - dim - 1))

    level = one(*split[0])
    for cut in split[1:]:
        level = level * one(*cut)
    return level


def shared_out(own_key, own, number, rows, count, top, reach, skew):
    order = jax.random.permutation(own_key, count)
    heavy_load, common = portions_of(count, rows * top, reach, skew, True), portions_of(count, rows * top, reach, skew, False)
    places = jnp.arange(count)

    def named(sizes, offset_by):
        used = int((sizes > 0).sum())
        fixed = max(1, used // 4)
        shifted = fixed + (places - fixed + offset_by * (used - fixed)) % max(1, count - fixed)
        return jnp.zeros((count,), jnp.int32).at[order[jnp.where(places < fixed, places, shifted)]].set(jnp.asarray(sizes, jnp.int32))

    sizes = jnp.where(number % 4 == 0, named(heavy_load, number // 4), named(common, number - number // 4 - 1))
    mixed = jax.random.permutation(jax.random.fold_in(own, 3), count)
    giver, receiver = mixed[0:count // 2 * 2:2], mixed[1:count // 2 * 2:2]
    room = jnp.minimum(sizes[giver] - 1, reach - sizes[receiver]) // 2
    room = jnp.where((giver == order[0]) | (receiver == order[0]) | (sizes[receiver] == 0), 0, jnp.maximum(room, 0))
    shifted = jax.random.randint(jax.random.fold_in(own, 4), (count // 2,), 0, 1 << 20) % (room + 1)
    sizes = sizes.at[giver].add(-shifted).at[receiver].add(shifted)
    members = jnp.searchsorted(jnp.cumsum(sizes), jnp.arange(rows * top), side="right").astype(jnp.int32)
    table = members.reshape(top, rows).T
    table = table[jax.random.permutation(jax.random.fold_in(own, 1), rows)]
    offset_by = jax.random.randint(jax.random.fold_in(own, 2), (rows, 1), 0, top)
    return jnp.take_along_axis(table, (jnp.arange(top)[None, :] + offset_by) % top, axis=1)


def portions_of(amount, total, most, lean, full):
    loads = [(1 << 20) // math.isqrt(grade ** lean) + 1 for grade in range(1, amount + 1)]
    largest = most if full else min(most, max(-(-total // amount), total * loads[0] // sum(loads)))
    least = 1 if total - largest >= amount - 1 else 0
    given, rest = [largest] + [least] * (amount - 1), total - largest - least * (amount - 1)
    while rest > 0:
        candidates = [i for i in range(1, amount) if given[i] < largest] or [i for i in range(1, amount) if given[i] < most]
        whole, remaining = sum([loads[i] for i in candidates]), rest
        for i in candidates:
            extra = min(most - given[i], max(1, remaining * loads[i] // whole), rest)
            given[i] = given[i] + extra
            rest = rest - extra
    return np.array(given)


def scatter_about(own_key, shape, width, reach, split=(), kind=jnp.bfloat16):
    drawn = jax.random.normal(own_key, shape, jnp.float32) * width
    if len(split) > 0:
        drawn = level_of(own_key, shape, split, -0.22, 0.18) * drawn
    return jnp.clip(drawn, min=-reach, max=reach).astype(kind)


def setup_inputs(seed: int = 0) -> dict:
    seeds = jax.random.split(jax.random.key(seed), 5)
    embeddings = scatter_about(seeds[0], (READ_ROWS, D), 1.0, 6.0, ((0, 128),))
    log_norms = jnp.clip(6.5 + 3.0 * jax.random.uniform(seeds[1], (READ_ROWS,), jnp.float32) ** level_of(seeds[1], (READ_ROWS,), ((0, 128),), -0.2, 0.2), 6.5, 9.5).astype(jnp.bfloat16)
    destinations_keys = jax.random.split(jax.random.fold_in(seeds[2], 1), READ_ROWS // POOL)
    destinations_turns = jax.random.permutation(jax.random.fold_in(seeds[2], 3), READ_ROWS // POOL)
    destinations = jax.vmap(lambda own, number: shared_out(jax.random.fold_in(seeds[2], 2), own, number, POOL, N_BLK, 1, CAP, 1))(destinations_keys, destinations_turns).reshape((READ_ROWS, 1))
    centroids = scatter_about(seeds[3], (CENTROIDS, D), 1.0, 6.0, ((0, 128),))
    return {"embeddings": embeddings, "log_norms": log_norms, "destinations": destinations, "centroids": centroids}


def contribute(panel, rows, lse, sums, counts):
    scale = rows.shape[1] ** -0.5
    scores = jnp.dot(rows, panel.T, preferred_element_type=jnp.float32) * scale
    resp = jnp.exp(scores - lse.astype(jnp.float32)[:, None])
    counts = counts + jnp.sum(resp, axis=0)
    resp_low = resp.astype(jnp.bfloat16)
    sums = sums + lax.dot_general(resp_low, rows, (((0,), (0,)), ((), ())), preferred_element_type=jnp.float32)
    return sums, counts


def reference(embeddings, log_norms, destinations, centroids):
    dest = destinations[:, 0].astype(jnp.int32)
    onehot = (dest[:, None] == jnp.arange(N_BLK, dtype=jnp.int32)[None, :]).astype(jnp.int32)
    rank = jnp.sum((jnp.cumsum(onehot, axis=0) - onehot) * onehot, axis=1).astype(jnp.int32)
    slots = N_BLK * CAP
    rows_buf = jnp.zeros((N_BLK, slots, D), embeddings.dtype).at[dest, rank].set(embeddings)
    lse_buf = jnp.full((N_BLK, slots), 1e4, log_norms.dtype).at[dest, rank].set(log_norms)
    panels = centroids.reshape(N_BLK, PANEL, D)

    def one_panel(index):
        panel = panels[index]
        sums = jnp.zeros((PANEL, D), jnp.float32)
        counts = jnp.zeros((PANEL,), jnp.float32)
        for stop in range(STOPS + 1):
            device = (index + stop) % N_BLK
            sums, counts = contribute(panel, rows_buf[device], lse_buf[device], sums, counts)
        fresh = (sums + panel.astype(jnp.float32)) / (counts + 1.0)[:, None]
        return fresh.astype(jnp.bfloat16)

    result = lax.map(one_panel, jnp.arange(N_BLK, dtype=jnp.int32))
    return result.reshape(N_BLK * PANEL, D)
```

```python
import functools

import jax
import jax.numpy as jnp
import ml_dtypes
import numpy as np
from jax import lax
from jax.experimental import pallas as pl
from jax.experimental.pallas import tpu as pltpu
from jax.sharding import PartitionSpec as P

MESH = pl.DeviceIdType.MESH
SIDE = 4
CAP = 5
EMPTY = 9984.0
GROUP = 16
CHUNKS = 6
BLOCK = 32
SLOTS = GROUP * CAP
TILE = 512


def hops(off):
    return sum(min(step, SIDE - step) for step in off)


OFFSETS = sorted(
    [(x, z, y) for x in range(SIDE) for z in range(SIDE) for y in range(SIDE) if x + z + y > 0],
    key=lambda off: -hops(off),
)


def packing():
    pack = np.zeros((GROUP * BLOCK, (CHUNKS + 1) * SLOTS), np.float32)
    for peer in range(GROUP):
        for slot in range(CAP):
            for chunk in range(CHUNKS):
                pack[peer * BLOCK + chunk * CAP + slot, chunk * SLOTS + peer * CAP + slot] = 1
            pack[peer * BLOCK + CHUNKS * CAP, CHUNKS * SLOTS + peer * CAP + slot] = 1
    lane = np.zeros((SLOTS, 128), np.float32)
    for row in range(SLOTS):
        lane[row, row % CAP] = 1
    return pack, lane


def kernel(
    rows_hbm, dest_hbm, lse_hbm, pack_hbm, unpack_hbm, lane_hbm, panel_hbm, out_hbm,
    rows, dest, lse, pack, unpack, lane, panel, out,
    stack, send, recv, swap, x_ref, l_ref, total, mass,
    in_sem, out_sem, send_sem, recv_sem, swap_send, swap_recv,
):
    me = lax.axis_index("blk")
    core = lax.rem(me, 2)
    chip = me // 2
    y = lax.rem(chip, SIDE)
    z = lax.rem(chip // SIDE, SIDE)
    x = chip // (SIDE * SIDE)
    other = me + 1 - 2 * core
    n = len(OFFSETS)
    devices = 2 * SIDE**3
    pool, width = rows.shape

    def chip_at(off):
        return (lax.rem(x + off[0], SIDE) * SIDE + lax.rem(z + off[1], SIDE)) * SIDE + lax.rem(y + off[2], SIDE)

    barrier = pltpu.get_barrier_semaphore()
    pl.semaphore_signal(barrier, inc=1, device_id=(other,), device_id_type=MESH)
    for off in OFFSETS:
        pl.semaphore_signal(barrier, inc=1, device_id=(2 * chip_at(off) + core,), device_id_type=MESH)

    loads = [
        pltpu.make_async_copy(src, dst, in_sem.at[i])
        for i, (src, dst) in enumerate(
            [(dest_hbm, dest), (rows_hbm, rows), (lse_hbm, lse), (pack_hbm, pack), (lane_hbm, lane), (unpack_hbm, unpack), (panel_hbm, panel)]
        )
    ]
    for load in loads:
        load.start()

    loads[0].wait()
    to = dest[...]
    hot = lax.broadcasted_iota(jnp.int32, (devices, pool), 0) == to
    earlier = lax.broadcasted_iota(jnp.int32, (pool, pool), 0) < lax.broadcasted_iota(jnp.int32, (pool, pool), 1)
    before = jnp.dot(hot.astype(jnp.bfloat16), earlier.astype(jnp.bfloat16), preferred_element_type=jnp.float32)
    rank = jnp.sum(jnp.where(hot, before, 0.0), axis=0, keepdims=True).astype(jnp.int32)
    slot = to * CAP + rank
    picks = lax.broadcasted_iota(jnp.int32, (devices * CAP, pool), 0) == slot
    loads[1].wait()
    sorted_rows = jnp.dot(picks.astype(jnp.bfloat16), rows[...], preferred_element_type=jnp.float32).astype(jnp.bfloat16)
    loads[2].wait()
    norm = lse[...].astype(jnp.float32) - EMPTY
    norms = jnp.sum(jnp.where(picks, norm, 0.0), axis=1, keepdims=True) + EMPTY
    loads[3].wait()
    loads[4].wait()
    for g in range(devices // GROUP):
        part = slice(g * SLOTS, (g + 1) * SLOTS)
        lanes = slice(g * 128, (g + 1) * 128)
        for j in range(CHUNKS):
            stack[j * SLOTS : (j + 1) * SLOTS, lanes] = sorted_rows[part, j * 128 : (j + 1) * 128]
        stack[CHUNKS * SLOTS :, lanes] = (norms[part] * lane[...].astype(jnp.float32)).astype(jnp.bfloat16)
    for h in range(devices // GROUP // 2):
        packed = jnp.dot(pack[...], stack[:, h * 256 : (h + 1) * 256], preferred_element_type=jnp.float32).astype(jnp.bfloat16)
        for i in range(2):
            g = 2 * h + i
            send[g * GROUP : (g + 1) * GROUP] = packed[:, i * 128 : (i + 1) * 128].reshape(GROUP, BLOCK, 128)
        if h == 0:
            send[devices : devices + 2] = packed[: 2 * BLOCK, :128].reshape(2, BLOCK, 128)

    pl.semaphore_wait(barrier, n + 1)
    for i, off in enumerate(OFFSETS):
        to_chip = chip_at(off)
        pltpu.make_async_remote_copy(
            src_ref=send.at[pl.ds(2 * to_chip, 4)],
            dst_ref=recv.at[i],
            send_sem=send_sem,
            recv_sem=recv_sem.at[i // GROUP],
            device_id=(2 * to_chip + core,),
            device_id_type=MESH,
        ).start()
    recv[n] = send[pl.ds(2 * chip, 4)]

    x_ref[...] = jnp.zeros_like(x_ref)
    empty = lax.broadcasted_iota(jnp.int32, (16, 128), 1) == 0
    l_ref[3 * SLOTS :] = jnp.where(empty, EMPTY, 0.0).astype(jnp.bfloat16)
    total[...] = jnp.zeros_like(total)
    mass[...] = jnp.zeros_like(mass)
    log2e = 1.4426950408889634
    scale = float(width) ** -0.5 * log2e
    loads[5].wait()
    loads[6].wait()

    def unpacked(block):
        packed = jnp.concatenate([block[:, d].reshape(GROUP * BLOCK, 128) for d in range(3)], axis=1)
        wide = jnp.dot(unpack[...], packed, preferred_element_type=jnp.float32).astype(jnp.bfloat16)
        for d in range(3):
            part = slice(d * SLOTS, (d + 1) * SLOTS)
            lanes = slice(d * 128, (d + 1) * 128)
            for j in range(CHUNKS):
                x_ref[part, j * 128 : (j + 1) * 128] = wide[j * SLOTS : (j + 1) * SLOTS, lanes]
            l_ref[part] = wide[CHUNKS * SLOTS :, lanes] * lane[...]
        norm = lax.dot_general(
            jnp.ones((8, 128), jnp.bfloat16), l_ref[...], (((1,), (1,)), ((), ())), preferred_element_type=jnp.float32
        )
        return norm[0:1] * log2e

    def contribute(block, last):
        norm = unpacked(block)
        xs = x_ref[...]
        for t in range(panel.shape[0] // TILE):
            tile = slice(t * TILE, (t + 1) * TILE)
            score = lax.dot_general(panel[tile], xs, (((1,), (1,)), ((), ())), preferred_element_type=jnp.float32)
            resp = jnp.exp2(score * scale - norm)
            count = resp[:, :128] + resp[:, 128:] + mass[tile]
            add = jnp.dot(resp.astype(jnp.bfloat16), xs, preferred_element_type=jnp.float32)
            if not last:
                mass[tile] = count
                total[tile] += add
            else:
                inverse = 1.0 / (jnp.sum(count, axis=1, keepdims=True) + 1.0)
                fresh = (total[tile] + add + panel[tile].astype(jnp.float32)) * inverse
                out[tile] = fresh.astype(jnp.bfloat16)
                pltpu.make_async_copy(out.at[tile], out_hbm.at[tile], out_sem.at[t]).start()

    groups = (n + 1) // GROUP
    for g in range(groups):
        arrived = recv.at[pl.ds(g * GROUP, GROUP if g < groups - 1 else GROUP - 1)]
        pltpu.make_async_copy(arrived, arrived, recv_sem.at[g]).wait()
        handed = pltpu.make_async_remote_copy(
            src_ref=recv.at[pl.ds(g * GROUP, GROUP), pl.ds(1 - core, 3)],
            dst_ref=swap.at[pl.ds(g * GROUP, GROUP)],
            send_sem=swap_send.at[g],
            recv_sem=swap_recv.at[g],
            device_id=(other,),
            device_id_type=MESH,
        )
        handed.start()
        contribute(recv[pl.ds(g * GROUP, GROUP), pl.ds(core, 3)], False)
        handed.wait()
        contribute(swap[pl.ds(g * GROUP, GROUP)], g == groups - 1)

    sent = recv.at[pl.ds(0, n)]
    pltpu.make_async_copy(sent, sent, send_sem).wait()
    for t in range(panel.shape[0] // TILE):
        tile = slice(t * TILE, (t + 1) * TILE)
        pltpu.make_async_copy(out.at[tile], out_hbm.at[tile], out_sem.at[t]).wait()


def body(embeddings, log_norms, destinations, centroids):
    devices = lax.axis_size("blk")
    pool, width = embeddings.shape
    panel = centroids.shape[0]
    pack, lane = packing()
    bf16 = jnp.bfloat16
    chips = len(OFFSETS) + 1
    groups = chips // GROUP
    any_spec = pl.BlockSpec(memory_space=pl.ANY)
    return pl.pallas_call(
        kernel,
        out_shape=jax.ShapeDtypeStruct((panel, width), bf16),
        in_specs=[any_spec] * 7,
        out_specs=any_spec,
        scratch_shapes=[
            pltpu.VMEM((pool, width), bf16),
            pltpu.VMEM((1, pool), jnp.int32),
            pltpu.VMEM((1, pool), jnp.float32),
            pltpu.VMEM(pack.shape, bf16),
            pltpu.VMEM(pack.shape[::-1], bf16),
            pltpu.VMEM(lane.shape, bf16),
            pltpu.VMEM((panel, width), bf16),
            pltpu.VMEM((panel, width), bf16),
            pltpu.VMEM(((CHUNKS + 1) * SLOTS, devices // GROUP * 128), bf16),
            pltpu.VMEM((devices + 2, BLOCK, 128), bf16),
            pltpu.VMEM((chips, 4, BLOCK, 128), bf16),
            pltpu.VMEM((chips, 3, BLOCK, 128), bf16),
            pltpu.VMEM((256, width), bf16),
            pltpu.VMEM((256, 128), bf16),
            pltpu.VMEM((panel, width), jnp.float32),
            pltpu.VMEM((panel, 128), jnp.float32),
            pltpu.SemaphoreType.DMA((7,)),
            pltpu.SemaphoreType.DMA((panel // TILE,)),
            pltpu.SemaphoreType.DMA,
            pltpu.SemaphoreType.DMA((groups,)),
            pltpu.SemaphoreType.DMA((groups,)),
            pltpu.SemaphoreType.DMA((groups,)),
        ],
        compiler_params=pltpu.CompilerParams(
            collective_id=0, has_side_effects=True, vmem_limit_bytes=48 * 2**20
        ),
        cost_estimate=pl.CostEstimate(
            flops=4 * 3 * CAP * devices * panel * width,
            bytes_accessed=4 * panel * width,
            transcendentals=3 * CAP * devices * panel,
        ),
    )(
        embeddings,
        destinations.reshape(1, pool),
        log_norms.astype(jnp.float32).reshape(1, pool),
        jnp.asarray(pack.astype(ml_dtypes.bfloat16)),
        jnp.asarray(pack.T.astype(ml_dtypes.bfloat16)),
        jnp.asarray(lane.astype(ml_dtypes.bfloat16)),
        centroids,
    )


def solution(mesh):
    return jax.shard_map(
        body,
        mesh=mesh,
        in_specs=(P("blk", None), P("blk"), P("blk", None), P("blk", None)),
        out_specs=P("blk", None),
        check_vma=False,
    )
```

```python
import jax
import jax.numpy as jnp
from jax import lax
from jax.experimental import pallas as pl
from jax.experimental.pallas import tpu as pltpu
from jax.sharding import PartitionSpec as P

MESH = pl.DeviceIdType.MESH
SIDE = 4
CAP = 5
EMPTY = 9984.0
GROUP = 16
CHUNKS = 6
BLOCK = 32
SLOTS = GROUP * CAP
TILE = 256
WINDOW = 2


def hops(off):
    return sum(min(step, SIDE - step) for step in off)


def ORDER(off):
    return (-sum(off) % SIDE == 0, sum(off) % SIDE, -hops(off))


OFFSETS = sorted(
    [(x, z, y) for x in range(SIDE) for z in range(SIDE) for y in range(SIDE) if x + z + y > 0],
    key=ORDER,
)


def packing(shape, stacked_dim):
    stacked = lax.broadcasted_iota(jnp.int32, shape, stacked_dim)
    chunk = sum([(stacked >= j * SLOTS).astype(jnp.int32) for j in range(1, CHUNKS + 1)])
    inside = stacked - chunk * SLOTS
    peer = (inside * 6554) >> 15
    row = jnp.where(chunk < CHUNKS, chunk * CAP + inside - peer * CAP, CHUNKS * CAP)
    return peer * BLOCK + row


def kernel(
    rows_hbm, dest_hbm, lse_hbm, panel_hbm, out_hbm,
    rows, dest, lse, pack, unpack, lane, panel, out,
    stack, send, recv, swap, x_ref, l_ref, total, mass,
    in_sem, out_sem, send_sem, recv_sem, swap_send, swap_recv,
):
    me = lax.axis_index("blk")
    core = lax.rem(me, 2)
    chip = me // 2
    y = lax.rem(chip, SIDE)
    z = lax.rem(chip // SIDE, SIDE)
    x = chip // (SIDE * SIDE)
    other = me + 1 - 2 * core
    n = len(OFFSETS)
    groups = (n + 1) // GROUP
    devices = 2 * SIDE**3
    pool, width = rows.shape

    def chip_at(off):
        return (lax.rem(x + off[0], SIDE) * SIDE + lax.rem(z + off[1], SIDE)) * SIDE + lax.rem(y + off[2], SIDE)

    barrier = pltpu.get_barrier_semaphore()
    pl.semaphore_signal(barrier, inc=1, device_id=(other,), device_id_type=MESH)
    for off in OFFSETS:
        pl.semaphore_signal(barrier, inc=1, device_id=(2 * chip_at(off) + core,), device_id_type=MESH)

    loads = [
        pltpu.make_async_copy(src, dst, in_sem.at[i])
        for i, (src, dst) in enumerate(
            [(dest_hbm, dest), (rows_hbm, rows), (lse_hbm, lse), (panel_hbm, panel)]
        )
    ]
    for load in loads:
        load.start()

    depth = (CHUNKS + 1) * SLOTS
    wide = GROUP * BLOCK
    stacked = packing((8, depth), 1)[0:1]
    pack[...] = (lax.broadcasted_iota(jnp.int32, (wide, depth), 0) == stacked).astype(jnp.bfloat16)
    stacked = packing((depth, 128), 0)[:, 0:1]
    unpack[...] = (lax.broadcasted_iota(jnp.int32, (depth, wide), 1) == stacked).astype(jnp.bfloat16)
    row = lax.broadcasted_iota(jnp.int32, (SLOTS, 128), 0)
    own_lane = lax.broadcasted_iota(jnp.int32, (SLOTS, 128), 1) == row - ((row * 6554) >> 15) * CAP
    lane[...] = own_lane.astype(jnp.bfloat16)

    loads[0].wait()
    to = dest[...]
    hot = lax.broadcasted_iota(jnp.int32, (devices, pool), 0) == to
    earlier = lax.broadcasted_iota(jnp.int32, (pool, pool), 0) < lax.broadcasted_iota(jnp.int32, (pool, pool), 1)
    before = jnp.dot(hot.astype(jnp.bfloat16), earlier.astype(jnp.bfloat16), preferred_element_type=jnp.float32)
    rank = jnp.sum(jnp.where(hot, before, 0.0), axis=0, keepdims=True).astype(jnp.int32)
    slot = to * CAP + rank
    picks = lax.broadcasted_iota(jnp.int32, (devices * CAP, pool), 0) == slot
    loads[1].wait()
    sorted_rows = jnp.dot(picks.astype(jnp.bfloat16), rows[...], preferred_element_type=jnp.float32).astype(jnp.bfloat16)
    loads[2].wait()
    norm = lse[...].astype(jnp.float32) - EMPTY
    norms = jnp.sum(jnp.where(picks, norm, 0.0), axis=1, keepdims=True) + EMPTY
    for g in range(devices // GROUP):
        part = slice(g * SLOTS, (g + 1) * SLOTS)
        lanes = slice(g * 128, (g + 1) * 128)
        for j in range(CHUNKS):
            stack[j * SLOTS : (j + 1) * SLOTS, lanes] = sorted_rows[part, j * 128 : (j + 1) * 128]
        stack[CHUNKS * SLOTS :, lanes] = (norms[part] * lane[...].astype(jnp.float32)).astype(jnp.bfloat16)
    for h in range(devices // GROUP // 2):
        packed = jnp.dot(pack[...], stack[:, h * 256 : (h + 1) * 256], preferred_element_type=jnp.float32).astype(jnp.bfloat16)
        for i in range(2):
            g = 2 * h + i
            send[g * GROUP : (g + 1) * GROUP] = packed[:, i * 128 : (i + 1) * 128].reshape(GROUP, BLOCK, 128)
        if h == 0:
            send[devices : devices + 2] = packed[: 2 * BLOCK, :128].reshape(2, BLOCK, 128)

    pl.semaphore_wait(barrier, n + 1)
    def dispatch(g):
        for i in range(g * GROUP, min((g + 1) * GROUP, n)):
            to_chip = chip_at(OFFSETS[i])
            pltpu.make_async_remote_copy(
                src_ref=send.at[pl.ds(2 * to_chip, 4)],
                dst_ref=recv.at[i],
                send_sem=send_sem,
                recv_sem=recv_sem.at[g],
                device_id=(2 * to_chip + core,),
                device_id_type=MESH,
            ).start()

    for g in range(WINDOW):
        dispatch(g)
    recv[n] = send[pl.ds(2 * chip, 4)]

    x_ref[...] = jnp.zeros_like(x_ref)
    empty = lax.broadcasted_iota(jnp.int32, (16, 128), 1) == 0
    l_ref[3 * SLOTS :] = jnp.where(empty, EMPTY, 0.0).astype(jnp.bfloat16)
    total[...] = jnp.zeros_like(total)
    mass[...] = jnp.zeros_like(mass)
    log2e = 1.4426950408889634
    scale = float(width) ** -0.5 * log2e
    loads[3].wait()

    def unpacked(block):
        packed = jnp.concatenate([block[:, d].reshape(GROUP * BLOCK, 128) for d in range(3)], axis=1)
        wide = jnp.dot(unpack[...], packed, preferred_element_type=jnp.float32).astype(jnp.bfloat16)
        for d in range(3):
            part = slice(d * SLOTS, (d + 1) * SLOTS)
            lanes = slice(d * 128, (d + 1) * 128)
            for j in range(CHUNKS):
                x_ref[part, j * 128 : (j + 1) * 128] = wide[j * SLOTS : (j + 1) * SLOTS, lanes]
            l_ref[part] = wide[CHUNKS * SLOTS :, lanes] * lane[...]
        norm = lax.dot_general(
            jnp.ones((8, 128), jnp.bfloat16), l_ref[...], (((1,), (1,)), ((), ())), preferred_element_type=jnp.float32
        )
        return norm[0:1] * log2e

    def contribute(block, last):
        norm = unpacked(block)
        xs = x_ref[...]
        for t in range(panel.shape[0] // TILE):
            tile = slice(t * TILE, (t + 1) * TILE)
            score = lax.dot_general(panel[tile], xs, (((1,), (1,)), ((), ())), preferred_element_type=jnp.float32)
            resp = jnp.exp2(score * scale - norm)
            count = resp[:, :128] + resp[:, 128:] + mass[tile]
            add = jnp.dot(resp.astype(jnp.bfloat16), xs, preferred_element_type=jnp.float32)
            if not last:
                mass[tile] = count
                total[tile] += add
            else:
                inverse = 1.0 / (jnp.sum(count, axis=1, keepdims=True) + 1.0)
                fresh = (total[tile] + add + panel[tile].astype(jnp.float32)) * inverse
                out[tile] = fresh.astype(jnp.bfloat16)
                pltpu.make_async_copy(out.at[tile], out_hbm.at[tile], out_sem.at[t]).start()

    for g in range(groups):
        arrived = recv.at[pl.ds(g * GROUP, GROUP if g < groups - 1 else GROUP - 1)]
        pltpu.make_async_copy(arrived, arrived, recv_sem.at[g]).wait()
        if g + WINDOW < groups:
            dispatch(g + WINDOW)
        handed = pltpu.make_async_remote_copy(
            src_ref=recv.at[pl.ds(g * GROUP, GROUP), pl.ds(1 - core, 3)],
            dst_ref=swap.at[pl.ds(g * GROUP, GROUP)],
            send_sem=swap_send.at[g],
            recv_sem=swap_recv.at[g],
            device_id=(other,),
            device_id_type=MESH,
        )
        handed.start()
        contribute(recv[pl.ds(g * GROUP, GROUP), pl.ds(core, 3)], False)
        handed.wait()
        contribute(swap[pl.ds(g * GROUP, GROUP)], g == groups - 1)

    sent = recv.at[pl.ds(0, n)]
    pltpu.make_async_copy(sent, sent, send_sem).wait()
    for t in range(panel.shape[0] // TILE):
        tile = slice(t * TILE, (t + 1) * TILE)
        pltpu.make_async_copy(out.at[tile], out_hbm.at[tile], out_sem.at[t]).wait()


def body(embeddings, log_norms, destinations, centroids):
    devices = lax.axis_size("blk")
    pool, width = embeddings.shape
    panel = centroids.shape[0]
    depth, wide = (CHUNKS + 1) * SLOTS, GROUP * BLOCK
    bf16 = jnp.bfloat16
    chips = len(OFFSETS) + 1
    groups = chips // GROUP
    any_spec = pl.BlockSpec(memory_space=pl.ANY)
    return pl.pallas_call(
        kernel,
        out_shape=jax.ShapeDtypeStruct((panel, width), bf16),
        in_specs=[any_spec] * 4,
        out_specs=any_spec,
        scratch_shapes=[
            pltpu.VMEM((pool, width), bf16),
            pltpu.VMEM((1, pool), jnp.int32),
            pltpu.VMEM((1, pool), jnp.float32),
            pltpu.VMEM((wide, depth), bf16),
            pltpu.VMEM((depth, wide), bf16),
            pltpu.VMEM((SLOTS, 128), bf16),
            pltpu.VMEM((panel, width), bf16),
            pltpu.VMEM((panel, width), bf16),
            pltpu.VMEM((depth, devices // GROUP * 128), bf16),
            pltpu.VMEM((devices + 2, BLOCK, 128), bf16),
            pltpu.VMEM((chips, 4, BLOCK, 128), bf16),
            pltpu.VMEM((chips, 3, BLOCK, 128), bf16),
            pltpu.VMEM((256, width), bf16),
            pltpu.VMEM((256, 128), bf16),
            pltpu.VMEM((panel, width), jnp.float32),
            pltpu.VMEM((panel, 128), jnp.float32),
            pltpu.SemaphoreType.DMA((4,)),
            pltpu.SemaphoreType.DMA((panel // TILE,)),
            pltpu.SemaphoreType.DMA,
            pltpu.SemaphoreType.DMA((groups,)),
            pltpu.SemaphoreType.DMA((groups,)),
            pltpu.SemaphoreType.DMA((groups,)),
        ],
        compiler_params=pltpu.CompilerParams(
            collective_id=0, has_side_effects=True, vmem_limit_bytes=63 * 2**20
        ),
        cost_estimate=pl.CostEstimate(
            flops=4 * 3 * CAP * devices * panel * width,
            bytes_accessed=4 * panel * width,
            transcendentals=3 * CAP * devices * panel,
        ),
    )(
        embeddings,
        destinations.reshape(1, pool),
        log_norms.astype(jnp.float32).reshape(1, pool),
        centroids,
    )


def solution(mesh):
    return jax.shard_map(
        body,
        mesh=mesh,
        in_specs=(P("blk", None), P("blk"), P("blk", None), P("blk", None)),
        out_specs=P("blk", None),
        check_vma=False,
    )
```

```python
import jax
import jax.numpy as jnp
from jax import lax
from jax.experimental import pallas as pl
from jax.experimental.pallas import tpu as pltpu
from jax.sharding import PartitionSpec as P

MESH = pl.DeviceIdType.MESH
SIDE = 4
CAP = 5
EMPTY = 9984.0
GROUP = 16
CHUNKS = 6
BLOCK = 32
SLOTS = GROUP * CAP
TILE = 256
WINDOW = 2


def hops(off):
    return sum(min(step, SIDE - step) for step in off)


def ORDER(off):
    return (-sum(off) % SIDE == 0, sum(off) % SIDE, -hops(off))


OFFSETS = sorted(
    [(x, z, y) for x in range(SIDE) for z in range(SIDE) for y in range(SIDE) if x + z + y > 0],
    key=ORDER,
)


def packing(shape, stacked_dim):
    stacked = lax.broadcasted_iota(jnp.int32, shape, stacked_dim)
    chunk = sum([(stacked >= j * SLOTS).astype(jnp.int32) for j in range(1, CHUNKS + 1)])
    inside = stacked - chunk * SLOTS
    peer = (inside * 6554) >> 15
    row = jnp.where(chunk < CHUNKS, chunk * CAP + inside - peer * CAP, CHUNKS * CAP)
    return peer * BLOCK + row


def kernel(
    rows_hbm, dest_hbm, lse_hbm, panel_hbm, out,
    rows, dest, lse, pack, unpack, lane, panel,
    stack, send, recv, swap, x_ref, l_ref, total, mass,
    in_sem, send_sem, recv_sem, swap_send, swap_recv,
):
    me = lax.axis_index("blk")
    core = lax.rem(me, 2)
    chip = me // 2
    y = lax.rem(chip, SIDE)
    z = lax.rem(chip // SIDE, SIDE)
    x = chip // (SIDE * SIDE)
    other = me + 1 - 2 * core
    n = len(OFFSETS)
    groups = (n + 1) // GROUP
    devices = 2 * SIDE**3
    pool, width = rows.shape

    def chip_at(off):
        a, b, c = (first + core * (second - first) for first, second in zip(off, off[1:] + off[:1]))
        return (lax.rem(x + a, SIDE) * SIDE + lax.rem(z + b, SIDE)) * SIDE + lax.rem(y + c, SIDE)

    barrier = pltpu.get_barrier_semaphore()
    pl.semaphore_signal(barrier, inc=1, device_id=(other,), device_id_type=MESH)
    for off in OFFSETS:
        pl.semaphore_signal(barrier, inc=1, device_id=(2 * chip_at(off) + core,), device_id_type=MESH)

    loads = [
        pltpu.make_async_copy(src, dst, in_sem.at[i])
        for i, (src, dst) in enumerate(
            [(dest_hbm, dest), (rows_hbm, rows), (lse_hbm, lse), (panel_hbm, panel)]
        )
    ]
    for load in loads:
        load.start()

    depth = (CHUNKS + 1) * SLOTS
    wide = GROUP * BLOCK
    stacked = packing((8, depth), 1)[0:1]
    pack[...] = (lax.broadcasted_iota(jnp.int32, (wide, depth), 0) == stacked).astype(jnp.bfloat16)
    stacked = packing((depth, 128), 0)[:, 0:1]
    unpack[...] = (lax.broadcasted_iota(jnp.int32, (depth, wide), 1) == stacked).astype(jnp.bfloat16)
    row = lax.broadcasted_iota(jnp.int32, (SLOTS, 128), 0)
    own_lane = lax.broadcasted_iota(jnp.int32, (SLOTS, 128), 1) == row - ((row * 6554) >> 15) * CAP
    lane[...] = own_lane.astype(jnp.bfloat16)

    loads[0].wait()
    to = dest[...]
    hot = lax.broadcasted_iota(jnp.int32, (devices, pool), 0) == to
    earlier = lax.broadcasted_iota(jnp.int32, (pool, pool), 0) < lax.broadcasted_iota(jnp.int32, (pool, pool), 1)
    before = jnp.dot(hot.astype(jnp.bfloat16), earlier.astype(jnp.bfloat16), preferred_element_type=jnp.float32)
    rank = jnp.sum(jnp.where(hot, before, 0.0), axis=0, keepdims=True).astype(jnp.int32)
    slot = to * CAP + rank
    picks = lax.broadcasted_iota(jnp.int32, (devices * CAP, pool), 0) == slot
    loads[1].wait()
    sorted_rows = jnp.dot(picks.astype(jnp.bfloat16), rows[...], preferred_element_type=jnp.float32).astype(jnp.bfloat16)
    loads[2].wait()
    norm = lse[...].reshape(1, pool).astype(jnp.float32) - EMPTY
    norms = jnp.sum(jnp.where(picks, norm, 0.0), axis=1, keepdims=True) + EMPTY
    for g in range(devices // GROUP):
        part = slice(g * SLOTS, (g + 1) * SLOTS)
        lanes = slice(g * 128, (g + 1) * 128)
        for j in range(CHUNKS):
            stack[j * SLOTS : (j + 1) * SLOTS, lanes] = sorted_rows[part, j * 128 : (j + 1) * 128]
        stack[CHUNKS * SLOTS :, lanes] = (norms[part] * lane[...].astype(jnp.float32)).astype(jnp.bfloat16)
    for h in range(devices // GROUP // 2):
        packed = jnp.dot(pack[...], stack[:, h * 256 : (h + 1) * 256], preferred_element_type=jnp.float32).astype(jnp.bfloat16)
        for i in range(2):
            g = 2 * h + i
            send[g * GROUP : (g + 1) * GROUP] = packed[:, i * 128 : (i + 1) * 128].reshape(GROUP, BLOCK, 128)
        if h == 0:
            send[devices : devices + 2] = packed[: 2 * BLOCK, :128].reshape(2, BLOCK, 128)

    pl.semaphore_wait(barrier, n + 1)
    def dispatch(g):
        for i in range(g * GROUP, min((g + 1) * GROUP, n)):
            to_chip = chip_at(OFFSETS[i])
            pltpu.make_async_remote_copy(
                src_ref=send.at[pl.ds(2 * to_chip, 4)],
                dst_ref=recv.at[i],
                send_sem=send_sem,
                recv_sem=recv_sem.at[g],
                device_id=(2 * to_chip + core,),
                device_id_type=MESH,
            ).start()

    for g in range(WINDOW):
        dispatch(g)
    recv[n] = send[pl.ds(2 * chip, 4)]

    x_ref[...] = jnp.zeros_like(x_ref)
    empty = lax.broadcasted_iota(jnp.int32, (16, 128), 1) == 0
    l_ref[3 * SLOTS :] = jnp.where(empty, EMPTY, 0.0).astype(jnp.bfloat16)
    total[...] = jnp.zeros_like(total)
    mass[...] = jnp.zeros_like(mass)
    log2e = 1.4426950408889634
    scale = float(width) ** -0.5 * log2e
    loads[3].wait()

    def unpacked(block):
        packed = jnp.concatenate([block[:, d].reshape(GROUP * BLOCK, 128) for d in range(3)], axis=1)
        wide = jnp.dot(unpack[...], packed, preferred_element_type=jnp.float32).astype(jnp.bfloat16)
        for d in range(3):
            part = slice(d * SLOTS, (d + 1) * SLOTS)
            lanes = slice(d * 128, (d + 1) * 128)
            for j in range(CHUNKS):
                x_ref[part, j * 128 : (j + 1) * 128] = wide[j * SLOTS : (j + 1) * SLOTS, lanes]
            l_ref[part] = wide[CHUNKS * SLOTS :, lanes] * lane[...]
        norm = lax.dot_general(
            jnp.ones((8, 128), jnp.bfloat16), l_ref[...], (((1,), (1,)), ((), ())), preferred_element_type=jnp.float32
        )
        return norm[0:1] * log2e

    def contribute(block, last):
        norm = unpacked(block)
        xs = x_ref[...]
        for t in range(panel.shape[0] // TILE):
            tile = slice(t * TILE, (t + 1) * TILE)
            score = lax.dot_general(panel[tile], xs, (((1,), (1,)), ((), ())), preferred_element_type=jnp.float32)
            resp = jnp.exp2(score * scale - norm)
            count = resp[:, :128] + resp[:, 128:] + mass[tile]
            add = jnp.dot(resp.astype(jnp.bfloat16), xs, preferred_element_type=jnp.float32)
            if not last:
                mass[tile] = count
                total[tile] += add
            else:
                inverse = 1.0 / (jnp.sum(count, axis=1, keepdims=True) + 1.0)
                fresh = (total[tile] + add + panel[tile].astype(jnp.float32)) * inverse
                out[tile] = fresh.astype(jnp.bfloat16)

    for g in range(groups):
        arrived = recv.at[pl.ds(g * GROUP, GROUP if g < groups - 1 else GROUP - 1)]
        pltpu.make_async_copy(arrived, arrived, recv_sem.at[g]).wait()
        if g + WINDOW < groups:
            dispatch(g + WINDOW)
        handed = pltpu.make_async_remote_copy(
            src_ref=recv.at[pl.ds(g * GROUP, GROUP), pl.ds(1 - core, 3)],
            dst_ref=swap.at[pl.ds(g * GROUP, GROUP)],
            send_sem=swap_send.at[g],
            recv_sem=swap_recv.at[g],
            device_id=(other,),
            device_id_type=MESH,
        )
        handed.start()
        contribute(recv[pl.ds(g * GROUP, GROUP), pl.ds(core, 3)], False)
        handed.wait()
        contribute(swap[pl.ds(g * GROUP, GROUP)], g == groups - 1)

    sent = recv.at[pl.ds(0, n)]
    pltpu.make_async_copy(sent, sent, send_sem).wait()


def body(embeddings, log_norms, destinations, centroids):
    devices = lax.axis_size("blk")
    pool, width = embeddings.shape
    panel = centroids.shape[0]
    depth, wide = (CHUNKS + 1) * SLOTS, GROUP * BLOCK
    bf16 = jnp.bfloat16
    chips = len(OFFSETS) + 1
    groups = chips // GROUP
    return pl.pallas_call(
        kernel,
        out_shape=jax.ShapeDtypeStruct((panel, width), bf16),
        in_specs=[pl.BlockSpec(memory_space=pl.ANY)] * 4,
        out_specs=pl.BlockSpec(memory_space=pltpu.VMEM),
        scratch_shapes=[
            pltpu.VMEM((pool, width), bf16),
            pltpu.VMEM((1, pool), jnp.int32),
            pltpu.VMEM((pool,), bf16),
            pltpu.VMEM((wide, depth), bf16),
            pltpu.VMEM((depth, wide), bf16),
            pltpu.VMEM((SLOTS, 128), bf16),
            pltpu.VMEM((panel, width), bf16),
            pltpu.VMEM((depth, devices // GROUP * 128), bf16),
            pltpu.VMEM((devices + 2, BLOCK, 128), bf16),
            pltpu.VMEM((chips, 4, BLOCK, 128), bf16),
            pltpu.VMEM((chips, 3, BLOCK, 128), bf16),
            pltpu.VMEM((256, width), bf16),
            pltpu.VMEM((256, 128), bf16),
            pltpu.VMEM((panel, width), jnp.float32),
            pltpu.VMEM((panel, 128), jnp.float32),
            pltpu.SemaphoreType.DMA((4,)),
            pltpu.SemaphoreType.DMA,
            pltpu.SemaphoreType.DMA((groups,)),
            pltpu.SemaphoreType.DMA((groups,)),
            pltpu.SemaphoreType.DMA((groups,)),
        ],
        compiler_params=pltpu.CompilerParams(
            collective_id=0, has_side_effects=True, vmem_limit_bytes=40 * 2**20
        ),
        cost_estimate=pl.CostEstimate(
            flops=4 * 3 * CAP * devices * panel * width,
            bytes_accessed=4 * panel * width,
            transcendentals=3 * CAP * devices * panel,
        ),
    )(
        *[
            pltpu.with_memory_space_constraint(operand, pltpu.HBM)
            for operand in (embeddings, destinations.reshape(1, pool), log_norms, centroids)
        ]
    )


def solution(mesh):
    return jax.shard_map(
        body,
        mesh=mesh,
        in_specs=(P("blk", None), P("blk"), P("blk", None), P("blk", None)),
        out_specs=P("blk", None),
        check_vma=False,
    )
```

```python
import jax
import jax.numpy as jnp
from jax import lax
from jax.experimental import pallas as pl
from jax.experimental.pallas import tpu as pltpu
from jax.sharding import PartitionSpec as P

MESH = pl.DeviceIdType.MESH
SIDE = 4
CAP = 5
EMPTY = 9984.0
GROUP = 16
CHUNKS = 6
BLOCK = 32
SLOTS = GROUP * CAP
TILE = 256
WINDOW = 2


def hops(off):
    return sum(min(step, SIDE - step) for step in off)


def ORDER(off):
    return (-sum(off) % SIDE == 0, sum(off) % SIDE, -hops(off))


OFFSETS = sorted(
    [(x, z, y) for x in range(SIDE) for z in range(SIDE) for y in range(SIDE) if x + z + y > 0],
    key=ORDER,
)


def packing(shape, stacked_dim):
    stacked = lax.broadcasted_iota(jnp.int32, shape, stacked_dim)
    chunk = sum([(stacked >= j * SLOTS).astype(jnp.int32) for j in range(1, CHUNKS + 1)])
    inside = stacked - chunk * SLOTS
    peer = (inside * 6554) >> 15
    row = jnp.where(chunk < CHUNKS, chunk * CAP + inside - peer * CAP, CHUNKS * CAP)
    return peer * BLOCK + row


def kernel(
    rows_hbm, dest_hbm, lse_hbm, panel_hbm, out,
    rows, dest, lse, pack, unpack, lane, panel,
    stack, send, recv, swap, x_ref, l_ref, total, mass,
    in_sem, send_sem, recv_sem, swap_send, swap_recv,
):
    me = lax.axis_index("blk")
    core = lax.rem(me, 2)
    chip = me // 2
    y = lax.rem(chip, SIDE)
    z = lax.rem(chip // SIDE, SIDE)
    x = chip // (SIDE * SIDE)
    other = me + 1 - 2 * core
    n = len(OFFSETS)
    groups = (n + 1) // GROUP
    devices = 2 * SIDE**3
    pool, width = rows.shape

    def chip_at(off):
        a, b, c = (first + core * (second - first) for first, second in zip(off, off[1:] + off[:1]))
        return (lax.rem(x + a, SIDE) * SIDE + lax.rem(z + b, SIDE)) * SIDE + lax.rem(y + c, SIDE)

    barrier = pltpu.get_barrier_semaphore()
    pl.semaphore_signal(barrier, inc=1, device_id=(other,), device_id_type=MESH)
    for off in OFFSETS:
        pl.semaphore_signal(barrier, inc=1, device_id=(2 * chip_at(off) + core,), device_id_type=MESH)

    loads = [
        pltpu.make_async_copy(src, dst, in_sem.at[i])
        for i, (src, dst) in enumerate(
            [(dest_hbm, dest), (rows_hbm, rows), (lse_hbm, lse), (panel_hbm, panel)]
        )
    ]
    for load in loads:
        load.start()

    depth = (CHUNKS + 1) * SLOTS
    wide = GROUP * BLOCK
    stacked = packing((8, depth), 1)[0:1]
    pack[...] = (lax.broadcasted_iota(jnp.int32, (wide, depth), 0) == stacked).astype(jnp.bfloat16)
    stacked = packing((depth, 128), 0)[:, 0:1]
    unpack[...] = (lax.broadcasted_iota(jnp.int32, (depth, wide), 1) == stacked).astype(jnp.bfloat16)
    row = lax.broadcasted_iota(jnp.int32, (SLOTS, 128), 0)
    own_lane = lax.broadcasted_iota(jnp.int32, (SLOTS, 128), 1) == row - ((row * 6554) >> 15) * CAP
    lane[...] = own_lane.astype(jnp.bfloat16)

    loads[0].wait()
    to = dest[...]
    hot = lax.broadcasted_iota(jnp.int32, (devices, pool), 0) == to
    earlier = lax.broadcasted_iota(jnp.int32, (pool, pool), 0) < lax.broadcasted_iota(jnp.int32, (pool, pool), 1)
    before = jnp.dot(hot.astype(jnp.bfloat16), earlier.astype(jnp.bfloat16), preferred_element_type=jnp.float32)
    rank = jnp.sum(jnp.where(hot, before, 0.0), axis=0, keepdims=True).astype(jnp.int32)
    slot = to * CAP + rank
    picks = lax.broadcasted_iota(jnp.int32, (devices * CAP, pool), 0) == slot
    loads[1].wait()
    sorted_rows = jnp.dot(picks.astype(jnp.bfloat16), rows[...], preferred_element_type=jnp.float32).astype(jnp.bfloat16)
    loads[2].wait()
    norm = lse[...].reshape(1, pool).astype(jnp.float32) - EMPTY
    norms = jnp.sum(jnp.where(picks, norm, 0.0), axis=1, keepdims=True) + EMPTY
    for g in range(devices // GROUP):
        part = slice(g * SLOTS, (g + 1) * SLOTS)
        lanes = slice(g * 128, (g + 1) * 128)
        for j in range(CHUNKS):
            stack[j * SLOTS : (j + 1) * SLOTS, lanes] = sorted_rows[part, j * 128 : (j + 1) * 128]
        stack[CHUNKS * SLOTS :, lanes] = (norms[part] * lane[...].astype(jnp.float32)).astype(jnp.bfloat16)
    for h in range(devices // GROUP // 2):
        packed = jnp.dot(pack[...], stack[:, h * 256 : (h + 1) * 256], preferred_element_type=jnp.float32).astype(jnp.bfloat16)
        for i in range(2):
            g = 2 * h + i
            send[g * GROUP : (g + 1) * GROUP] = packed[:, i * 128 : (i + 1) * 128].reshape(GROUP, BLOCK, 128)
        if h == 0:
            send[devices : devices + 2] = packed[: 2 * BLOCK, :128].reshape(2, BLOCK, 128)

    pl.semaphore_wait(barrier, n + 1)
    def dispatch(g):
        for i in range(g * GROUP, min((g + 1) * GROUP, n)):
            to_chip = chip_at(OFFSETS[i])
            pltpu.make_async_remote_copy(
                src_ref=send.at[pl.ds(2 * to_chip, 4)],
                dst_ref=recv.at[i],
                send_sem=send_sem,
                recv_sem=recv_sem.at[g],
                device_id=(2 * to_chip + core,),
                device_id_type=MESH,
            ).start()

    for g in range(WINDOW):
        dispatch(g)
    recv[n] = send[pl.ds(2 * chip, 4)]

    x_ref[...] = jnp.zeros_like(x_ref)
    empty = lax.broadcasted_iota(jnp.int32, (16, 128), 1) == 0
    l_ref[3 * SLOTS :] = jnp.where(empty, EMPTY, 0.0).astype(jnp.bfloat16)
    total[...] = jnp.zeros_like(total)
    mass[...] = jnp.zeros_like(mass)
    log2e = 1.4426950408889634
    scale = float(width) ** -0.5 * log2e
    loads[3].wait()

    def unpacked(block):
        packed = jnp.concatenate([block[:, d].reshape(GROUP * BLOCK, 128) for d in range(3)], axis=1)
        wide = jnp.dot(unpack[...], packed, preferred_element_type=jnp.float32).astype(jnp.bfloat16)
        for d in range(3):
            part = slice(d * SLOTS, (d + 1) * SLOTS)
            lanes = slice(d * 128, (d + 1) * 128)
            for j in range(CHUNKS):
                x_ref[part, j * 128 : (j + 1) * 128] = wide[j * SLOTS : (j + 1) * SLOTS, lanes]
            l_ref[part] = wide[CHUNKS * SLOTS :, lanes] * lane[...]
        norm = lax.dot_general(
            jnp.ones((8, 128), jnp.bfloat16), l_ref[...], (((1,), (1,)), ((), ())), preferred_element_type=jnp.float32
        )
        return norm[0:1] * log2e

    def contribute(block, last):
        norm = unpacked(block)
        xs = x_ref[...]

        def scores(t):
            if t == panel.shape[0] // TILE:
                return None
            rows_of = panel[t * TILE : (t + 1) * TILE]
            return lax.dot_general(rows_of, xs, (((1,), (1,)), ((), ())), preferred_element_type=jnp.float32)

        ahead = scores(0)
        for t in range(panel.shape[0] // TILE):
            tile = slice(t * TILE, (t + 1) * TILE)
            score, ahead = ahead, scores(t + 1)
            resp = jnp.exp2(score * scale - norm)
            count = resp[:, :128] + resp[:, 128:] + mass[tile]
            add = jnp.dot(resp.astype(jnp.bfloat16), xs, preferred_element_type=jnp.float32)
            if not last:
                mass[tile] = count
                total[tile] += add
            else:
                inverse = 1.0 / (jnp.sum(count, axis=1, keepdims=True) + 1.0)
                fresh = (total[tile] + add + panel[tile].astype(jnp.float32)) * inverse
                out[tile] = fresh.astype(jnp.bfloat16)

    for g in range(groups):
        arrived = recv.at[pl.ds(g * GROUP, GROUP if g < groups - 1 else GROUP - 1)]
        pltpu.make_async_copy(arrived, arrived, recv_sem.at[g]).wait()
        if g + WINDOW < groups:
            dispatch(g + WINDOW)
        handed = pltpu.make_async_remote_copy(
            src_ref=recv.at[pl.ds(g * GROUP, GROUP), pl.ds(1 - core, 3)],
            dst_ref=swap.at[pl.ds(g * GROUP, GROUP)],
            send_sem=swap_send.at[g],
            recv_sem=swap_recv.at[g],
            device_id=(other,),
            device_id_type=MESH,
        )
        handed.start()
        contribute(recv[pl.ds(g * GROUP, GROUP), pl.ds(core, 3)], False)
        handed.wait()
        contribute(swap[pl.ds(g * GROUP, GROUP)], g == groups - 1)

    sent = recv.at[pl.ds(0, n)]
    pltpu.make_async_copy(sent, sent, send_sem).wait()


def body(embeddings, log_norms, destinations, centroids):
    devices = lax.axis_size("blk")
    pool, width = embeddings.shape
    panel = centroids.shape[0]
    depth, wide = (CHUNKS + 1) * SLOTS, GROUP * BLOCK
    bf16 = jnp.bfloat16
    chips = len(OFFSETS) + 1
    groups = chips // GROUP
    return pl.pallas_call(
        kernel,
        out_shape=jax.ShapeDtypeStruct((panel, width), bf16),
        in_specs=[pl.BlockSpec(memory_space=pl.ANY)] * 4,
        out_specs=pl.BlockSpec(memory_space=pltpu.VMEM),
        scratch_shapes=[
            pltpu.VMEM((pool, width), bf16),
            pltpu.VMEM((1, pool), jnp.int32),
            pltpu.VMEM((pool,), bf16),
            pltpu.VMEM((wide, depth), bf16),
            pltpu.VMEM((depth, wide), bf16),
            pltpu.VMEM((SLOTS, 128), bf16),
            pltpu.VMEM((panel, width), bf16),
            pltpu.VMEM((depth, devices // GROUP * 128), bf16),
            pltpu.VMEM((devices + 2, BLOCK, 128), bf16),
            pltpu.VMEM((chips, 4, BLOCK, 128), bf16),
            pltpu.VMEM((chips, 3, BLOCK, 128), bf16),
            pltpu.VMEM((256, width), bf16),
            pltpu.VMEM((256, 128), bf16),
            pltpu.VMEM((panel, width), jnp.float32),
            pltpu.VMEM((panel, 128), jnp.float32),
            pltpu.SemaphoreType.DMA((4,)),
            pltpu.SemaphoreType.DMA,
            pltpu.SemaphoreType.DMA((groups,)),
            pltpu.SemaphoreType.DMA((groups,)),
            pltpu.SemaphoreType.DMA((groups,)),
        ],
        compiler_params=pltpu.CompilerParams(
            collective_id=0, has_side_effects=True, vmem_limit_bytes=40 * 2**20
        ),
        cost_estimate=pl.CostEstimate(
            flops=4 * 3 * CAP * devices * panel * width,
            bytes_accessed=4 * panel * width,
            transcendentals=3 * CAP * devices * panel,
        ),
    )(
        *[
            pltpu.with_memory_space_constraint(operand, pltpu.HBM)
            for operand in (embeddings, destinations.reshape(1, pool), log_norms, centroids)
        ]
    )


def solution(mesh):
    return jax.shard_map(
        body,
        mesh=mesh,
        in_specs=(P("blk", None), P("blk"), P("blk", None), P("blk", None)),
        out_specs=P("blk", None),
        check_vma=False,
    )
```
